512 devices in a mesh: nodes: 64 (over z, x, core), hid: 8 (over y).
Axes of the slice: x: 4, y: 8, z: 8, core: 2. Of those that a mesh axis runs over, the one named last changes fastest.
Arguments:
- latents: bfloat16 [16384, 512], P('nodes'), may hold values from -16 to 16
- cotangent: bfloat16 [16384, 512], P('nodes'), may hold values from -16 to 16
- w_send: bfloat16 [512, 2048], P(None, 'hid'), may hold values from -0.1875 to 0.1875
- w_recv: bfloat16 [512, 2048], P(None, 'hid'), may hold values from -0.1875 to 0.1875
- bias: float32 [2048], P('hid'), may hold values from -1 to 1
- w_out: bfloat16 [2048, 512], P('hid'), may hold values from -0.125 to 0.125
- fine_sender: int32 [98304], P('nodes'), may hold values from 0 to 383
- fine_receiver: int32 [98304], P('nodes'), may hold values from 0 to 255
- fine_valid: int32 [98304], P('nodes'), may hold values from 0 to 1, as said below
- send_rows: int32 [64, 64, 4], P('nodes'), may hold values from 0 to 7
- coarse_slot: int32 [32768], P('nodes'), may hold values from 0 to 255
- coarse_receiver: int32 [32768], P('nodes'), may hold values from 0 to 255
- coarse_valid: int32 [32768], P('nodes'), may hold values from 0 to 1, as said below
Outputs:
- grad_nodes: float32 [16384, 512], P('nodes', 'hid')
- grad_send: float32 [512, 2048], P('nodes', 'hid')
- grad_recv: float32 [512, 2048], P('nodes', 'hid')
- grad_out: float32 [2048, 512], P('hid', 'nodes')
- grad_bias: float32 [2048], P(('hid', 'nodes'))
The draws below stay inside these ranges and needn't reach their ends.
Inputs may be any that keep to these rules, and one draw needn't show every extreme that they name: `fine_sender`: index into the receiving block's nodes extended by 64 nodes of the previous block in front and 64 of the next block behind. `fine_valid`: 1 marks a live edge, 0 a padding slot. `send_rows`: a node among the first 8 of block b. `coarse_slot`: slot q names the row that block q // 4 sends to the edge's block in its slot q % 4. `coarse_valid`: 1 marks a live edge, 0 a padding slot.
All inputs are finite; a program needn't handle non-finite values.
Results may differ from the reference program's by a relative error of at most 0.0065.
Values may be sent and summed in bfloat16 or wider, within the bound.
A program may use at most 64 MiB of HBM per device.

```python
import jax
import jax.numpy as jnp
from jax import lax

D = 512
HIDDEN_ALL = 2048
NODE_DEV = 256
COARSE_NODES = 8
COARSE_CAP = 4
FINE_DEV = 1536
COARSE_DEV = 512
HALO = 64
SLOTS = 256
NODES = 16384
FINE_EDGES = 98304
COARSE_EDGES = 32768
N_NODES = 64


def live_edges(key, per_block):
    key_level, key_value = jax.random.split(key)
    level = jax.random.randint(key_level, (N_NODES, 1), 35, 101)
    values = jax.random.randint(key_value, (N_NODES, per_block), 0, 100)
    return (values < level).astype(jnp.int32).reshape(-1)


def draw_fine_valid(key, part):
    key = jax.random.fold_in(key, 11)
    return live_edges(key, FINE_DEV)


def draw_coarse_valid(key, part):
    key = jax.random.fold_in(key, 23)
    return live_edges(key, COARSE_DEV)


def set_ends(drawn, key, smallest, largest):
    longest = drawn.shape.index(max(drawn.shape))
    spots = []
    for shift in (0, 1):
        where = [jax.random.randint(jax.random.fold_in(key, axis), (), 0, length) for axis, length in enumerate(drawn.shape)]
        where[longest] = (where[longest] + shift) % drawn.shape[longest]
        spots.append(tuple(where))
    return drawn.at[spots[0]].set(smallest).at[spots[1]].set(largest)


def strengthened(result, key, source, target, blocks, factor):
    owner, partner = [(jnp.arange(result.shape[position]) // (result.shape[position] // blocks)).reshape([-1 if axis == position else 1 for axis in range(result.ndim)]) for position in (source, target)]
    chosen = jax.random.permutation(key, blocks)[partner]
    strong = (owner == chosen) | (owner == (partner + blocks // 2) % blocks)
    return jnp.where(strong, factor * result, result)


def shard_levels(rng, dims, cuts, smallest, top_value):
    factor_of, own = 1.0, jax.random.fold_in(rng, 6)
    for axis_at, parts in cuts:
        heights = jnp.exp(jax.random.uniform(jax.random.fold_in(own, axis_at), (parts,), jnp.float32, smallest / len(cuts), top_value / len(cuts)))
        factor_of = factor_of * jnp.repeat(heights, dims[axis_at] // parts).reshape([-1 if axis == axis_at else 1 for axis in range(len(dims))])
    return factor_of


def bell_draw(rng, dims, width, limit, shards=(), kind=jnp.bfloat16):
    values = jax.random.normal(rng, dims, jnp.float32) * width
    if len(shards) > 0:
        values = shard_levels(rng, dims, shards, -0.22, 0.18) * values
    return jnp.clip(values, min=-limit, max=limit).astype(kind)


def gaussian_with(rng, extent, scale, reach, cuts, heavy, kind=jnp.bfloat16):
    entries = scale * jax.random.normal(rng, extent, jnp.float32)
    if cuts:
        entries = entries * shard_levels(rng, extent, cuts, -0.22, 0.18)
    return jnp.clip(strengthened(entries, jax.random.fold_in(rng, 3), *heavy), -reach, reach).astype(kind)


def setup_inputs(seed: int = 0) -> dict:
    key_list = jax.random.split(jax.random.key(seed), 14)
    latents = gaussian_with(key_list[0], (NODES, D), 1.0, 16.0, ((0, 64),), (0, 1, 64, 4.0))
    cotangent = gaussian_with(key_list[1], (NODES, D), 1.0, 16.0, ((0, 64),), (0, 1, 64, 4.0))
    w_send = bell_draw(key_list[2], (D, HIDDEN_ALL), (2 * D) ** -0.5, 0.1875, ((1, 8),))
    w_recv = bell_draw(key_list[3], (D, HIDDEN_ALL), (2 * D) ** -0.5, 0.1875, ((1, 8),))
    bias = jnp.clip(jax.random.uniform(key_list[4], (HIDDEN_ALL,), jnp.float32, -1.0, 1.0) * shard_levels(key_list[4], (HIDDEN_ALL,), ((0, 8),), -0.4, 0.0), -1.0, 1.0)
    w_out = bell_draw(key_list[5], (HIDDEN_ALL, D), HIDDEN_ALL ** -0.5, 0.125, ((0, 8),))
    fine_sender = set_ends(jax.random.randint(key_list[6], (FINE_EDGES,), 0, NODE_DEV + 2 * HALO), jax.random.fold_in(key_list[6], 1), 0, (NODE_DEV + 2 * HALO) - 1).astype(jnp.int32)
    fine_receiver = set_ends(jax.random.randint(key_list[7], (FINE_EDGES,), 0, NODE_DEV), jax.random.fold_in(key_list[7], 1), 0, NODE_DEV - 1).astype(jnp.int32)
    fine_valid = draw_fine_valid(jax.random.fold_in(key_list[13], 71), 0)
    send_rows = set_ends(jax.random.randint(key_list[9], (N_NODES, N_NODES, COARSE_CAP), 0, COARSE_NODES), jax.random.fold_in(key_list[9], 1), 0, COARSE_NODES - 1).astype(jnp.int32)
    coarse_slot = set_ends(jax.random.randint(key_list[10], (COARSE_EDGES,), 0, SLOTS), jax.random.fold_in(key_list[10], 1), 0, SLOTS - 1).astype(jnp.int32)
    coarse_receiver = set_ends(jax.random.randint(key_list[11], (COARSE_EDGES,), 0, NODE_DEV), jax.random.fold_in(key_list[11], 1), 0, NODE_DEV - 1).astype(jnp.int32)
    coarse_valid = draw_coarse_valid(jax.random.fold_in(key_list[13], 71), 0)
    return dict(latents=latents, cotangent=cotangent, w_send=w_send, w_recv=w_recv, bias=bias, w_out=w_out, fine_sender=fine_sender, fine_receiver=fine_receiver, fine_valid=fine_valid, send_rows=send_rows, coarse_slot=coarse_slot, coarse_receiver=coarse_receiver, coarse_valid=coarse_valid)


def reference(latents, cotangent, w_send, w_recv, bias, w_out, fine_sender, fine_receiver, fine_valid, send_rows, coarse_slot, coarse_receiver, coarse_valid):
    zero_rows = jnp.zeros((HALO, D), jnp.bfloat16)
    padded = jnp.concatenate([zero_rows, latents, zero_rows], 0)
    fine_send = fine_sender.reshape(N_NODES, FINE_DEV)
    fine_recv = fine_receiver.reshape(N_NODES, FINE_DEV)
    fine_live = fine_valid.reshape(N_NODES, FINE_DEV)
    coarse_rows = coarse_slot.reshape(N_NODES, COARSE_DEV)
    coarse_recv = coarse_receiver.reshape(N_NODES, COARSE_DEV)
    coarse_live = coarse_valid.reshape(N_NODES, COARSE_DEV)

    def device_step(totals, device):
        grad_pad, grad_send, grad_recv, grad_out, grad_bias = totals
        slots = lax.dynamic_index_in_dim(coarse_rows, device, 0, False)
        owners = lax.dynamic_index_in_dim(send_rows, device, 1, False)
        source_block = slots // COARSE_CAP
        coarse_node = source_block * NODE_DEV + owners[source_block, slots % COARSE_CAP]
        sender_index = jnp.concatenate([device * NODE_DEV + lax.dynamic_index_in_dim(fine_send, device, 0, False), HALO + coarse_node])
        local_recv = jnp.concatenate([lax.dynamic_index_in_dim(fine_recv, device, 0, False), lax.dynamic_index_in_dim(coarse_recv, device, 0, False)])
        receiver_index = HALO + device * NODE_DEV + local_recv
        live_mask = jnp.concatenate([lax.dynamic_index_in_dim(fine_live, device, 0, False), lax.dynamic_index_in_dim(coarse_live, device, 0, False)])
        senders = padded[sender_index]
        receivers = padded[receiver_index]
        preact = jnp.dot(senders, w_send, preferred_element_type=jnp.float32) + jnp.dot(receivers, w_recv, preferred_element_type=jnp.float32) + bias
        hidden = jax.nn.silu(preact).astype(jnp.bfloat16)
        upstream = cotangent[receiver_index - HALO] * live_mask[:, None].astype(jnp.bfloat16)
        backed = jnp.dot(upstream, w_out.T, preferred_element_type=jnp.float32)
        sigmoid_pre = jax.nn.sigmoid(preact)
        grad_pre = (backed * sigmoid_pre * (1.0 + preact * (1.0 - sigmoid_pre))).astype(jnp.bfloat16)
        grad_out = grad_out + jnp.dot(hidden.T, upstream, preferred_element_type=jnp.float32)
        grad_send = grad_send + jnp.dot(senders.T, grad_pre, preferred_element_type=jnp.float32)
        grad_recv = grad_recv + jnp.dot(receivers.T, grad_pre, preferred_element_type=jnp.float32)
        grad_bias = grad_bias + jnp.sum(grad_pre.astype(jnp.float32), 0)
        sender_part = jnp.dot(grad_pre, w_send.T, preferred_element_type=jnp.float32)
        receiver_part = jnp.dot(grad_pre, w_recv.T, preferred_element_type=jnp.float32)
        grad_pad = grad_pad.at[sender_index].add(sender_part).at[receiver_index].add(receiver_part)
        return (grad_pad, grad_send, grad_recv, grad_out, grad_bias), None

    start = (jnp.zeros((NODES + 2 * HALO, D), jnp.float32), jnp.zeros((D, HIDDEN_ALL), jnp.float32), jnp.zeros((D, HIDDEN_ALL), jnp.float32), jnp.zeros((HIDDEN_ALL, D), jnp.float32), jnp.zeros((HIDDEN_ALL,), jnp.float32))
    totals, unused = lax.scan(device_step, start, jnp.arange(N_NODES, dtype=jnp.int32))
    grad_pad, grad_send, grad_recv, grad_out, grad_bias = totals
    grad_nodes = cotangent.astype(jnp.float32) + grad_pad[HALO:HALO + NODES]
    return (grad_nodes, grad_send, grad_recv, grad_out, grad_bias)
```

```python
import jax
import jax.numpy as jnp
from jax import lax
from jax.experimental import pallas as pl
from jax.experimental.pallas import tpu as pltpu
from jax.sharding import PartitionSpec as P

BF = jnp.bfloat16
F32 = jnp.float32
MESH = pl.DeviceIdType.MESH
NODES = 64
HID = 8
ZS, XS = 8, 4
ROWS = 256
D = 512
H = 256
HALO = 64
FINE = 1536
COARSE = 512
CH = 512
TILES = (8, 9, 8)


def nn(a, b):
    return lax.dot_general(a, b, (((1,), (0,)), ((), ())), preferred_element_type=F32)


def nt(a, b):
    return lax.dot_general(a, b, (((1,), (1,)), ((), ())), preferred_element_type=F32)


def split(v):
    hi = v.astype(BF)
    return hi, (v - hi.astype(F32)).astype(BF)


def one_hot(count, row):
    return (lax.broadcasted_iota(jnp.int32, (count, row.shape[1]), 0) == row).astype(F32).astype(BF)


def eye(n):
    a = lax.broadcasted_iota(jnp.int32, (n, n), 0)
    b = lax.broadcasted_iota(jnp.int32, (n, n), 1)
    return (a == b).astype(F32).astype(BF)


def kernel(
    lat_h, cot_h, ws_h, wr_h, bias_h, wo_h, fs_h, fr_h, fv_h, sr_h, cs_h, cr_h, cv_h,
    rz0, rz1, rz2, own_h, node_h, rcy,
    low, lat, cot, ws, wr, bias, wo, fs, fr, fv, sr, cs, cr, cv, load_sem,
    msg32, zrow, zrow32, zraw, zraw32, pick_s, pick_t, psel, prow, praw_s, praw_r, halo, wst, latt, cott, a_src, a_rcv, a_slot,
    g_src, g_rh, g_slot,
    ret_s, ret_r, col_s, col_r, rim_s, rim_r,
    buf0, buf1, buf2, rc0, rc1, rc2, xs0, xs1, xs2, rx0, rx1, rx2, sums, own, zs0, zs1, zs2,
    part, ys, ry, node_v, cy,
    zg_sem, pg_sem, zr_sem, pr_sem, halo_sem, rp_sem, rz_sem, rim_sem, core_sem, x_sem, z_sem, y_sem, cy_sem, out_sem,
):
    b = lax.axis_index("nodes")
    y = lax.axis_index("hid")
    c = lax.rem(b, 2)
    x = lax.rem(b // 2, XS)
    z = b // (2 * XS)
    bar = pltpu.get_barrier_semaphore()

    loads = [
        pltpu.make_async_copy(src, dst, load_sem.at[i])
        for i, (src, dst) in enumerate(
            (
                (sr_h, sr), (ws_h, ws), (lat_h, lat), (wr_h, wr), (cot_h, cot), (wo_h, wo), (bias_h, bias),
                (fs_h, fs), (fr_h, fr), (fv_h, fv), (cs_h, cs), (cr_h, cr), (cv_h, cv),
            )
        )
    ]
    first = pltpu.make_async_copy(lat_h.at[0:16], low, load_sem.at[13])
    first.start()
    for load in loads[0:2]:
        load.start()

    def block(zz, xx, cc):
        return (zz * XS + xx) * 2 + cc

    def plane(m, sign):
        return block(z, lax.rem(x + XS + sign * (m // 2), XS), lax.rem(c + m % 2, 2))

    def column(k, sign):
        return block(lax.rem(z + ZS + sign * k, ZS), x, c)

    def greet(**device):
        pl.semaphore_signal(bar, inc=1, device_id=device, device_id_type=MESH)

    for k in (4, 3, 5, 2, 6, 1, 7):
        greet(nodes=column(k, 1))
    for m in (4, 5, 2, 3, 6, 7, 1):
        greet(nodes=plane(m, 1))
    greet(nodes=lax.rem(b + NODES - 1 + 2 * c, NODES))
    for k in (4, 3, 5, 2, 6, 1, 7):
        greet(hid=lax.rem(y + k, HID))
    for load in loads[2:]:
        load.start()

    def remote(src, dst, sems, at, **device):
        return pltpu.make_async_remote_copy(
            src_ref=src, dst_ref=dst, send_sem=sems.at[0, at], recv_sem=sems.at[1, at],
            device_id=device, device_id_type=MESH,
        )

    msg32[...] = jnp.zeros_like(msg32)
    loads[0].wait()
    msg32[16:20, 0:NODES] = sr[...].astype(F32)
    first.wait()
    low32 = low[...].astype(F32)
    for k in range(4):
        zraw32[0, 8 * k : 8 * k + 8, :] = low32[0:8, 128 * k : 128 * k + 128]
    zraw[0] = zraw32[0].astype(BF)
    loads[1].wait()
    ahead = nn(low[...], ws[...])
    for k in range(2):
        msg32[8 * k : 8 * k + 8, :] = ahead[0:8, 128 * k : 128 * k + 128]
    zrow[0] = msg32[...].astype(BF)

    pl.semaphore_wait(bar, 22)

    z_rows = [remote(zrow.at[0], zrow.at[k], zg_sem, k - 1, nodes=column(k, 1)) for k in (4, 3, 5, 2, 6, 1, 7)]
    for copy in z_rows:
        copy.start()
    loads[2].wait()
    up = lax.rem(b + 1, NODES)
    down = lax.rem(b + NODES - 1, NODES)
    halos = (
        remote(lat.at[ROWS - HALO : ROWS], halo.at[0:HALO], halo_sem, 0, nodes=up),
        remote(lat.at[0:HALO], halo.at[HALO : 2 * HALO], halo_sem, 1, nodes=down),
    )
    for copy in halos:
        copy.start()

    z_raws = [remote(zraw.at[0], zraw.at[k], zr_sem, k - 1, nodes=column(k, 1)) for k in (4, 3, 5, 2, 6, 1, 7)]
    for copy in z_raws:
        copy.start()

    for load in loads[3:]:
        load.wait()
    eye256 = eye(256)
    wst[...] = nt(eye256, ws[...]).astype(BF)
    wrt = nt(eye256, wr[...]).astype(BF)
    bias_row = bias[...]
    b0 = bias_row.astype(BF)
    rest = bias_row - b0.astype(F32)
    b1 = rest.astype(BF)
    b2 = (rest - b1.astype(F32)).astype(BF)
    b_rows = jnp.concatenate([b0.astype(F32), b1.astype(F32), b2.astype(F32), jnp.zeros((5, H), F32)], 0)
    bias_col = jnp.sum(nt(eye256, b_rows.astype(BF)), axis=1, keepdims=True)
    for k in range(2):
        latt[256 * k : 256 * k + 256, 0:ROWS] = nt(eye256, lat[:, 256 * k : 256 * k + 256]).astype(BF)
        cott[256 * k : 256 * k + 256, :] = nt(eye256, cot[:, 256 * k : 256 * k + 256]).astype(BF)
    hi, lo = split(nn(wst[...], latt[:, 0:ROWS]))
    a_src[0:H, 0:ROWS] = hi
    a_src[H : 2 * H, 0:ROWS] = lo
    hi, lo = split(nn(wrt, latt[:, 0:ROWS]) + bias_col)
    a_rcv[0:H, :] = hi
    a_rcv[H : 2 * H, :] = lo
    a_rcv[2 * H : 3 * H, :] = nt(wo[...], cot[...]).astype(BF)

    wide = lax.broadcasted_iota(jnp.int32, (256, 128), 0)
    lane = lax.broadcasted_iota(jnp.int32, (256, 128), 1)
    spread = (lane == (wide & 7) * 16 + ((wide >> 3) & 3)).astype(F32).astype(BF)
    asked = ((z * XS + ((x + (wide >> 6)) & (XS - 1))) << 1) + ((c + (wide >> 5)) & 1)
    here = lane == asked
    for copy in z_rows:
        copy.wait()
    zrow32[...] = zrow[...].astype(F32)
    table = zrow32[:, 16:32, :].reshape(ZS * 16, 128).astype(BF)
    wanted = jnp.sum(jnp.where(here, nn(spread, table), 0.0), axis=1, keepdims=True)
    tall = lax.broadcasted_iota(jnp.int32, (256, 64), 0)
    node = lax.broadcasted_iota(jnp.int32, (256, 64), 1)
    chosen = ((node >> 3) == (tall & 7)) & ((node & 7).astype(F32) == wanted)
    pick_s[...] = chosen.astype(F32).astype(BF)
    for k in range(2):
        rows = zrow32[:, 8 * k : 8 * k + 8, :].reshape(64, 128).astype(BF)
        psel[:, :, 128 * k : 128 * k + 128] = nn(pick_s[...], rows).astype(BF).reshape(8, 32, 128)
    p_rows = [remote(psel.at[m], prow.at[m], pg_sem, m - 1, nodes=plane(m, 1)) for m in (4, 5, 2, 3, 6, 7, 1)]
    for copy in p_rows:
        copy.start()
    prow[0] = psel[0]
    pick_t[...] = nt(eye(64), pick_s[...]).astype(BF)

    for copy in halos:
        copy.wait()
    row = lax.broadcasted_iota(jnp.int32, (2 * HALO, D), 0)
    outside = ((row < HALO) & (b == 0)) | ((row >= HALO) & (b == NODES - 1))
    rim = jnp.where(outside, 0.0, halo[...].astype(F32)).astype(BF)
    for k in range(2):
        latt[256 * k : 256 * k + 256, ROWS : ROWS + 2 * HALO] = nt(eye256, rim[:, 256 * k : 256 * k + 256]).astype(BF)
    hi, lo = split(nn(wst[...], latt[:, ROWS : ROWS + 2 * HALO]))
    a_src[0:H, ROWS : ROWS + 2 * HALO] = hi
    a_src[H : 2 * H, ROWS : ROWS + 2 * HALO] = lo

    def edges(source, send_row, recv_row, live_row, count, exact):
        pick_s = one_hot(count, send_row)
        pick_r = one_hot(ROWS, recv_row)
        from_s = nn(source[...], pick_s)
        from_r = nn(a_rcv[...], pick_r)
        live = live_row.astype(F32)
        pre = from_s[0:H] + from_r[0:H] + from_r[H : 2 * H]
        if exact:
            pre += from_s[H : 2 * H]
        sig = 0.5 + 0.5 * jnp.tanh(0.5 * pre)
        act = pre * sig
        slope = sig + act * (1.0 - sig)
        grad = (from_r[2 * H :] * live * slope).astype(BF)
        hidden = (act * live).astype(BF)
        return pick_s, pick_r, grad, hidden

    for k in range(FINE // CH):
        at = slice(k * CH, (k + 1) * CH)
        s = fs[at].reshape(1, CH)
        s = jnp.where(s < HALO, s + ROWS, jnp.where(s < HALO + ROWS, s - HALO, s))
        by_s, by_r, grad, hidden = edges(a_src, s, fr[at].reshape(1, CH), fv[at].reshape(1, CH), ROWS + 2 * HALO, True)
        add_s, add_r = nt(by_s, grad), nt(by_r, jnp.concatenate([grad, hidden], 0))
        if k == 0:
            g_src[...] = add_s
            g_rh[...] = add_r
        else:
            g_src[...] += add_s
            g_rh[...] += add_r
        if k == 0:
            for copy in z_raws:
                copy.wait()
            zraw32[...] = zraw[...].astype(F32)
            for i in range(4):
                rows = zraw32[:, 8 * i : 8 * i + 8, :].reshape(64, 128).astype(BF)
                praw_s[:, :, 128 * i : 128 * i + 128] = nn(pick_s[...], rows).astype(BF).reshape(8, 32, 128)
            p_raws = [
                remote(praw_s.at[m], praw_r.at[m], pr_sem, m - 1, nodes=plane(m, 1)) for m in (4, 5, 2, 3, 6, 7, 1)
            ]
            for copy in p_raws:
                copy.start()
            praw_r[0] = praw_s[0]

    rim_s[...] = g_src[ROWS : ROWS + 2 * HALO, :].astype(BF)
    rims = (
        remote(rim_s.at[0:HALO], rim_r.at[HALO : 2 * HALO], rim_sem, 0, nodes=down),
        remote(rim_s.at[HALO : 2 * HALO], rim_r.at[0:HALO], rim_sem, 1, nodes=up),
    )
    for copy in rims:
        copy.start()

    for copy in p_rows:
        copy.wait()
    a_slot[...] = nt(eye256, prow[...].reshape(256, H)).astype(BF)
    q = cs[...]
    place = (
        (((x + XS - ((q >> 3) & (XS - 1))) & (XS - 1)) << 6)
        + (((c + (q >> 2)) & 1) << 5)
        + ((q & 3) << 3)
        + ((z + ZS - (q >> 5)) & (ZS - 1))
    )
    by_s, by_r, grad, hidden = edges(a_slot, place, cr[...], cv[...], 256, False)

    bufs, rcs, xss, rxs = (buf0, buf1, buf2), (rc0, rc1, rc2), (xs0, xs1, xs2), (rx0, rx1, rx2)
    zss, rzs = (zs0, zs1, zs2), (rz0, rz1, rz2)

    def lay_out(buf, value):
        for d in range(NODES):
            piece = value[8 * d : 8 * d + 8, :]
            tile = jnp.concatenate([piece[:, 0:128], piece[:, 128:256]], 0)
            buf[d % 2, (d // 2) % XS, d // (2 * XS)] = tile.astype(BF)

    cores = []

    def send_core(a):
        copy = remote(bufs[a].at[1 - c], rcs[a], core_sem, a, nodes=b + 1 - 2 * c)
        copy.start()
        cores.append(copy)

    x_copies = []

    def send_x(a):
        cores[a].wait()
        xss[a][...] = (bufs[a][c].astype(F32) + rcs[a][...].astype(F32)).astype(BF)
        for k in (2, 1, 3):
            to = lax.rem(x + k, XS)
            copy = remote(
                xss[a].at[to], rxs[a].at[k - 1], x_sem, 3 * a + k - 1, nodes=(z * XS + to) * 2 + c
            )
            copy.start()
            x_copies.append(copy)

    lay_out(buf0, nn(cott[...], (g_rh[:, H : 2 * H] + nt(by_r, hidden)).astype(BF)))
    send_core(0)

    g_slot[...] = nt(by_s, grad).astype(BF)
    ret_s[...] = g_slot[...].reshape(8, 32, H)
    backs = [remote(ret_s.at[m], ret_r.at[m], rp_sem, m - 1, nodes=plane(m, -1)) for m in (4, 5, 2, 3, 6, 7, 1)]
    for copy in backs:
        copy.start()
    ret_r[0] = ret_s[0]

    g_recv = g_rh[:, 0:H] + nt(by_r, grad)
    lay_out(buf1, nn(latt[:, 0:ROWS], g_recv.astype(BF)))
    total = jnp.sum(g_recv, axis=0, keepdims=True)
    bias_tile = jnp.concatenate([total[:, 0:128], total[:, 128:256], jnp.zeros((14, 128), F32)], 0).astype(BF)
    for i in range(2):
        for k in range(XS):
            buf1[i, k, 8] = bias_tile
    send_core(1)
    send_x(0)
    for copy in p_raws:
        copy.wait()
    arr = praw_r[...].reshape(256, D)
    for k in range(2):
        latt[256 * k : 256 * k + 256, 384:640] = nt(eye256, arr[:, 256 * k : 256 * k + 256]).astype(BF)
    lay_out(
        buf2,
        nn(latt[:, 0 : ROWS + 2 * HALO], g_src[...].astype(BF)) + nn(latt[:, 384:640], g_slot[...]),
    )
    send_core(2)
    send_x(1)

    for copy in rims:
        copy.wait()
    low = jnp.where(b == 0, 0.0, rim_r[0:HALO, :].astype(F32))
    high = jnp.where(b == NODES - 1, 0.0, rim_r[HALO : 2 * HALO, :].astype(F32))
    g_src[0:HALO, :] += low
    g_src[ROWS - HALO : ROWS, :] += high
    node = nt(ws[...], g_src[0:ROWS, :].astype(BF)) + nt(wr[...], g_recv.astype(BF))
    part[...] = node.reshape(HID, 64, ROWS)
    ys[...] = node.astype(BF).reshape(HID, 64, ROWS)
    y_copies = []
    for k in (4, 3, 5, 2, 6, 1, 7):
        to = lax.rem(y + k, HID)
        copy = remote(ys.at[to], ry.at[k - 1], y_sem, k - 1, hid=to)
        copy.start()
        y_copies.append(copy)

    send_x(2)

    for copy in backs:
        copy.wait()
    col_s[...] = nn(pick_t[...], ret_r[...].reshape(256, H)).reshape(ZS, 8, H)
    cols = [remote(col_s.at[k], col_r.at[k], rz_sem, k - 1, nodes=column(k, -1)) for k in (4, 3, 5, 2, 6, 1, 7)]
    for copy in cols:
        copy.start()
    col_r[0] = col_s[0]

    z_copies = []
    for a in range(3):
        for copy in x_copies[3 * a : 3 * a + 3]:
            copy.wait()
        mine = bufs[a][c, x].astype(F32) + rcs[a][x].astype(F32)
        for k in range(3):
            mine += rxs[a][k].astype(F32)
        sums[0:8] = mine[0:8]
        own[a] = sums[z]
        zss[a][:, 0:16, :] = mine[0:8].astype(BF)
        if a == 1:
            own[3] = mine[8]
            for k in range(ZS):
                zss[a][k, 16:32, :] = mine[8].astype(BF)
        for k in (4, 3, 5, 2, 6, 1, 7):
            to = lax.rem(z + k, ZS)
            copy = remote(
                zss[a].at[to], rzs[a].at[k - 1], z_sem, 7 * a + k - 1, nodes=(to * XS + x) * 2 + c
            )
            copy.start()
            z_copies.append(copy)

    own_out = pltpu.make_async_copy(own, own_h, out_sem.at[0])
    own_out.start()

    for copy in cols:
        copy.wait()
    coarse = col_r[0]
    for k in range(1, ZS):
        coarse += col_r[k]
    coarse = jnp.concatenate([coarse, jnp.zeros((8, H), F32)], 0)
    hi, lo = split(coarse)
    coarse_part = nt(hi, ws[...]) + nt(lo, ws[...])
    for k in range(HID):
        cy[k] = coarse_part[0:8, 128 * (k // 2) : 128 * (k // 2) + 128]
    cy_copies = []
    for k in (4, 3, 5, 2, 6, 1, 7):
        to = lax.rem(y + k, HID)
        copy = remote(cy.at[to], rcy.at[k - 1], cy_sem, k - 1, hid=to)
        copy.start()
        cy_copies.append(copy)

    cy_out = pltpu.make_async_copy(cy.at[y], rcy.at[HID - 1], out_sem.at[1])
    cy_out.start()

    for copy in y_copies:
        copy.wait()
    mine = part[y] + cott[pl.ds(pl.multiple_of(y * 64, 64), 64), :].astype(F32)
    for k in range(HID - 1):
        mine += ry[k].astype(F32)
    node_v[...] = mine
    node_out = pltpu.make_async_copy(node_v, node_h, out_sem.at[2])
    node_out.start()

    for copy in z_copies + cy_copies + [own_out, cy_out, node_out]:
        copy.wait()


def finish(
    rz0_h, rz1_h, rz2_h, own_h, node_h, rcy_h,
    n_out, s_out, r_out, o_out, b_out,
    rz0, rz1, rz2, own, node, rcy, n_v, s_v, r_v, o_v, in_sem, out_sem,
):
    b = lax.axis_index("nodes")
    y = lax.axis_index("hid")
    reads = [
        pltpu.make_async_copy(src, dst, in_sem.at[i])
        for i, (src, dst) in enumerate(
            ((own_h, own), (rz0_h, rz0), (rz1_h, rz1), (rz2_h, rz2), (rcy_h, rcy), (node_h, node))
        )
    ]
    for copy in reads:
        copy.start()
    writes = []

    def write(i, src, dst):
        copy = pltpu.make_async_copy(src, dst, out_sem.at[i])
        copy.start()
        writes.append(copy)

    reads[0].wait()
    for a, (rz, vec, out) in enumerate(((rz0, o_v, o_out), (rz1, r_v, r_out), (rz2, s_v, s_out))):
        reads[1 + a].wait()
        tile = own[a]
        for k in range(ZS - 1):
            tile += rz[k, 0:16].astype(F32)
        vec[...] = jnp.concatenate([tile[0:8], tile[8:16]], 1)
        write(a, vec, out)
    tile = own[3]
    for k in range(ZS - 1):
        tile += rz1[k, 16:32].astype(F32)
    line = jnp.broadcast_to(jnp.where(b < NODES // 2, tile[0:1], tile[1:2]), (8, 128))
    lane = lax.broadcasted_iota(jnp.int32, (128, 128), 0)
    want = lax.broadcasted_iota(jnp.int32, (128, 128), 1) + 4 * lax.rem(b, NODES // 2)
    take = (lane == want).astype(F32).astype(BF)
    v0 = line.astype(BF)
    rest = line - v0.astype(F32)
    v1 = rest.astype(BF)
    v2 = (rest - v1.astype(F32)).astype(BF)
    b_out[...] = (nn(v0, take) + nn(v1, take) + nn(v2, take))[0, 0:4]

    reads[4].wait()
    late = rcy[HID - 1]
    for k in range(HID - 1):
        late += rcy[k]
    late = jnp.concatenate([late, jnp.zeros((120, 128), F32)], 0).T
    late = jnp.where(lax.rem(y, 2) == 0, late[0:64, :], late[64:128, :])
    reads[5].wait()
    n_v[:, 0:128] = node[:, 0:128] + late
    n_v[:, 128:256] = node[:, 128:256]
    write(3, n_v, n_out)
    for copy in writes:
        copy.wait()


def vm(shape, dtype):
    return pltpu.VMEM(shape, dtype)


def shards(
    latents, cotangent, w_send, w_recv, bias, w_out, fine_sender, fine_receiver, fine_valid,
    send_rows, coarse_slot, coarse_receiver, coarse_valid,
):
    i32 = jnp.int32
    operands = (
        latents, cotangent, w_send, w_recv, bias.reshape(1, H), w_out,
        fine_sender, fine_receiver, fine_valid,
        send_rows[0].T,
        coarse_slot.reshape(1, COARSE), coarse_receiver.reshape(1, COARSE), coarse_valid.reshape(1, COARSE),
    )
    sems = pltpu.SemaphoreType.DMA
    scratch = [vm((16, D), BF)] + [vm(v.shape, v.dtype) for v in operands] + [sems((14,))]
    scratch += [
        vm((32, 128), F32), vm((ZS, 32, 128), BF), vm((ZS, 32, 128), F32), vm((ZS, 32, 128), BF),
        vm((ZS, 32, 128), F32), vm((256, 64), BF), vm((64, 256), BF),
        vm((8, 32, H), BF), vm((8, 32, H), BF), vm((8, 32, D), BF), vm((8, 32, D), BF),
        vm((2 * HALO, D), BF), vm((H, D), BF), vm((D, 640), BF), vm((D, ROWS), BF),
        vm((2 * H, 384), BF), vm((3 * H, ROWS), BF), vm((H, 256), BF),
        vm((384, H), F32), vm((ROWS, 2 * H), F32), vm((256, H), BF),
        vm((8, 32, H), BF), vm((8, 32, H), BF), vm((ZS, 8, H), F32), vm((ZS, 8, H), F32),
        vm((2 * HALO, H), BF), vm((2 * HALO, H), BF),
    ]
    scratch += [vm((2, XS, t, 16, 128), BF) for t in TILES]
    scratch += [vm((XS, t, 16, 128), BF) for t in TILES]
    scratch += [vm((XS, t, 16, 128), BF) for t in TILES]
    scratch += [vm((XS - 1, t, 16, 128), BF) for t in TILES]
    scratch += [vm((ZS, 16, 128), F32), vm((4, 16, 128), F32)]
    scratch += [vm((ZS, 16 * (t - 7), 128), BF) for t in TILES]
    scratch += [
        vm((HID, 64, ROWS), F32), vm((HID, 64, ROWS), BF), vm((HID - 1, 64, ROWS), BF),
        vm((64, ROWS), F32), vm((HID, 8, 128), F32),
    ]
    scratch += [
        sems((2, 7)), sems((2, 7)), sems((2, 7)), sems((2, 7)), sems((2, 2)), sems((2, 7)), sems((2, 7)), sems((2, 2)), sems((2, 3)), sems((2, 9)), sems((2, 21)),
        sems((2, 7)), sems((2, 7)), sems((3,)),
    ]
    hbm = pl.BlockSpec(memory_space=pltpu.MemorySpace.HBM)
    kept = [
        ((ZS - 1, 16, 128), BF), ((ZS - 1, 32, 128), BF), ((ZS - 1, 16, 128), BF),
        ((4, 16, 128), F32), ((64, ROWS), F32), ((HID, 8, 128), F32),
    ]
    arrived = pl.pallas_call(
        kernel,
        out_shape=[jax.ShapeDtypeStruct(shape, dtype) for shape, dtype in kept],
        in_specs=[hbm] * 13,
        out_specs=[hbm] * 6,
        scratch_shapes=scratch,
        compiler_params=pltpu.CompilerParams(
            collective_id=0, has_side_effects=True, vmem_limit_bytes=64 * 1024 * 1024
        ),
        name="edge_update",
    )(*operands)
    results = [(64, ROWS), (8, H), (8, H), (8, H)]
    out_n, out_s, out_r, out_o, out_b = pl.pallas_call(
        finish,
        out_shape=[jax.ShapeDtypeStruct(shape, F32) for shape in results + [(4,)]],
        in_specs=[hbm] * 6,
        out_specs=[hbm] * 4 + [pl.BlockSpec(memory_space=pltpu.VMEM)],
        scratch_shapes=[vm(shape, dtype) for shape, dtype in kept]
        + [vm(shape, F32) for shape in results]
        + [sems((6,)), sems((4,))],
        compiler_params=pltpu.CompilerParams(vmem_limit_bytes=64 * 1024 * 1024),
        name="finish",
    )(*arrived)
    return out_n.T, out_s, out_r, out_o.T, out_b


def solution(mesh):
    return jax.shard_map(
        shards,
        mesh=mesh,
        in_specs=(
            P("nodes", None), P("nodes", None), P(None, "hid"), P(None, "hid"), P("hid"), P("hid", None),
            P("nodes"), P("nodes"), P("nodes"), P("nodes", None, None), P("nodes"), P("nodes"), P("nodes"),
        ),
        out_specs=(
            P("nodes", "hid"), P("nodes", "hid"), P("nodes", "hid"), P("hid", "nodes"), P(("hid", "nodes")),
        ),
        check_vma=False,
    )
```

```python
import jax
import jax.numpy as jnp
from jax import lax
from jax.experimental import pallas as pl
from jax.experimental.pallas import tpu as pltpu
from jax.sharding import PartitionSpec as P

BF = jnp.bfloat16
F32 = jnp.float32
MESH = pl.DeviceIdType.MESH
NODES = 64
HID = 8
ZS, XS = 8, 4
ROWS = 256
D = 512
H = 256
HALO = 64
FINE = 1536
COARSE = 512
CH = 512
TILES = (8, 9, 8)


def nn(a, b):
    return lax.dot_general(a, b, (((1,), (0,)), ((), ())), preferred_element_type=F32)


def nt(a, b):
    return lax.dot_general(a, b, (((1,), (1,)), ((), ())), preferred_element_type=F32)


def split(v):
    hi = v.astype(BF)
    return hi, (v - hi.astype(F32)).astype(BF)


def one_hot(count, row):
    return (lax.broadcasted_iota(jnp.int32, (count, row.shape[1]), 0) == row).astype(F32).astype(BF)


def eye(n):
    a = lax.broadcasted_iota(jnp.int32, (n, n), 0)
    b = lax.broadcasted_iota(jnp.int32, (n, n), 1)
    return (a == b).astype(F32).astype(BF)


def kernel(
    lat_h, cot_h, ws_h, wr_h, bias_h, wo_h, fs_h, fr_h, fv_h, sr_h, cs_h, cr_h, cv_h,
    rz0, rz1, rz2, own_h, node_h, rcy,
    low, lat, cot, ws, wr, bias, wo, fs, fr, fv, sr, cs, cr, cv, load_sem,
    msg32, zrow, zrow32, zraw, zraw32, pick_s, pick_t, psel, prow, praw_s, praw_r, halo, wst, latt, cott, a_src, a_rcv, a_slot, oh_s, oh_r, oh_c, pre_in, back_in,
    g_src, g_rh, g_slot,
    ret_s, ret_r, col_s, col_r, rim_s, rim_r,
    buf0, buf1, buf2, rc0, rc1, rc2, xs0, xs1, xs2, rx0, rx1, rx2, sums, own, zs0, zs1, zs2,
    part, ys, ry, node_v, cy,
    zg_sem, pg_sem, zr_sem, pr_sem, halo_sem, rp_sem, rz_sem, rim_sem, core_sem, x_sem, z_sem, y_sem, cy_sem, out_sem,
):
    b = lax.axis_index("nodes")
    y = lax.axis_index("hid")
    c = lax.rem(b, 2)
    x = lax.rem(b // 2, XS)
    z = b // (2 * XS)
    bar = pltpu.get_barrier_semaphore()

    loads = [
        pltpu.make_async_copy(src, dst, load_sem.at[i])
        for i, (src, dst) in enumerate(
            (
                (sr_h, sr), (ws_h, ws), (lat_h, lat), (wr_h, wr), (cot_h, cot), (wo_h, wo), (bias_h, bias),
                (fs_h, fs), (fr_h, fr), (fv_h, fv), (cs_h, cs), (cr_h, cr), (cv_h, cv),
            )
        )
    ]
    first = pltpu.make_async_copy(lat_h.at[0:16], low, load_sem.at[13])
    first.start()
    for load in loads[0:2]:
        load.start()

    def block(zz, xx, cc):
        return (zz * XS + xx) * 2 + cc

    def plane(m, sign):
        return block(z, lax.rem(x + XS + sign * (m // 2), XS), lax.rem(c + m % 2, 2))

    def column(k, sign):
        return block(lax.rem(z + ZS + sign * k, ZS), x, c)

    def greet(**device):
        pl.semaphore_signal(bar, inc=1, device_id=device, device_id_type=MESH)

    for k in (4, 3, 5, 2, 6, 1, 7):
        greet(nodes=column(k, 1))
    for m in (4, 5, 2, 3, 6, 7, 1):
        greet(nodes=plane(m, 1))
    greet(nodes=lax.rem(b + NODES - 1 + 2 * c, NODES))
    for k in (4, 3, 5, 2, 6, 1, 7):
        greet(hid=lax.rem(y + k, HID))
    for load in loads[2:]:
        load.start()

    def remote(src, dst, sems, at, **device):
        return pltpu.make_async_remote_copy(
            src_ref=src, dst_ref=dst, send_sem=sems.at[0, at], recv_sem=sems.at[1, at],
            device_id=device, device_id_type=MESH,
        )

    msg32[...] = jnp.zeros_like(msg32)
    loads[0].wait()
    msg32[16:20, 0:NODES] = sr[...].astype(F32)
    first.wait()
    low32 = low[...].astype(F32)
    for k in range(4):
        zraw32[0, 8 * k : 8 * k + 8, :] = low32[0:8, 128 * k : 128 * k + 128]
    zraw[0] = zraw32[0].astype(BF)
    loads[1].wait()
    ahead = nn(low[...], ws[...])
    for k in range(2):
        msg32[8 * k : 8 * k + 8, :] = ahead[0:8, 128 * k : 128 * k + 128]
    zrow[0] = msg32[...].astype(BF)

    pl.semaphore_wait(bar, 22)

    z_rows = [remote(zrow.at[0], zrow.at[k], zg_sem, k - 1, nodes=column(k, 1)) for k in (4, 3, 5, 2, 6, 1, 7)]
    for copy in z_rows:
        copy.start()
    loads[2].wait()
    up = lax.rem(b + 1, NODES)
    down = lax.rem(b + NODES - 1, NODES)
    halos = (
        remote(lat.at[ROWS - HALO : ROWS], halo.at[0:HALO], halo_sem, 0, nodes=up),
        remote(lat.at[0:HALO], halo.at[HALO : 2 * HALO], halo_sem, 1, nodes=down),
    )
    for copy in halos:
        copy.start()

    z_raws = [remote(zraw.at[0], zraw.at[k], zr_sem, k - 1, nodes=column(k, 1)) for k in (4, 3, 5, 2, 6, 1, 7)]
    for copy in z_raws:
        copy.start()

    for load in loads[3:]:
        load.wait()
    eye256 = eye(256)
    wst[...] = nt(eye256, ws[...]).astype(BF)
    wrt = nt(eye256, wr[...]).astype(BF)
    bias_row = bias[...]
    b0 = bias_row.astype(BF)
    rest = bias_row - b0.astype(F32)
    b1 = rest.astype(BF)
    b2 = (rest - b1.astype(F32)).astype(BF)
    b_rows = jnp.concatenate([b0.astype(F32), b1.astype(F32), b2.astype(F32), jnp.zeros((5, H), F32)], 0)
    bias_col = jnp.sum(nt(eye256, b_rows.astype(BF)), axis=1, keepdims=True)
    for k in range(2):
        latt[256 * k : 256 * k + 256, 0:ROWS] = nt(eye256, lat[:, 256 * k : 256 * k + 256]).astype(BF)
        cott[256 * k : 256 * k + 256, :] = nt(eye256, cot[:, 256 * k : 256 * k + 256]).astype(BF)
    hi, lo = split(nn(wst[...], latt[:, 0:ROWS]))
    a_src[0:H, 0:ROWS] = hi
    a_src[H : 2 * H, 0:ROWS] = lo
    hi, lo = split(nn(wrt, latt[:, 0:ROWS]) + bias_col)
    a_rcv[0:H, :] = hi
    a_rcv[H : 2 * H, :] = lo
    a_rcv[2 * H : 3 * H, :] = nt(wo[...], cot[...]).astype(BF)

    for k in range(4):
        at = slice(k * CH, (k + 1) * CH)
        ends, live = (fr[at], fv[at]) if k < 3 else (cr[0, :], cv[0, :])
        oh_r[k] = one_hot(ROWS, ends.reshape(1, CH))
        from_r = nn(a_rcv[...], oh_r[k])
        back_in[k] = from_r[2 * H :] * live.reshape(1, CH).astype(F32)
        pre = from_r[0:H] + from_r[H : 2 * H]
        if k < 3:
            s = fs[at].reshape(1, CH)
            s = jnp.where(s < HALO, s + ROWS, jnp.where(s < HALO + ROWS, s - HALO, s))
            oh_s[k] = one_hot(ROWS + 2 * HALO, s)
            from_s = nn(a_src[:, 0:ROWS], oh_s[k, 0:ROWS, :])
            pre += from_s[0:H] + from_s[H : 2 * H]
        pre_in[k] = pre

    wide = lax.broadcasted_iota(jnp.int32, (256, 128), 0)
    lane = lax.broadcasted_iota(jnp.int32, (256, 128), 1)
    spread = (lane == (wide & 7) * 16 + ((wide >> 3) & 3)).astype(F32).astype(BF)
    asked = ((z * XS + ((x + (wide >> 6)) & (XS - 1))) << 1) + ((c + (wide >> 5)) & 1)
    here = lane == asked
    q = cs[...]
    place = (
        (((x + XS - ((q >> 3) & (XS - 1))) & (XS - 1)) << 6)
        + (((c + (q >> 2)) & 1) << 5)
        + ((q & 3) << 3)
        + ((z + ZS - (q >> 5)) & (ZS - 1))
    )
    oh_c[...] = one_hot(256, place)

    for copy in z_rows:
        copy.wait()
    zrow32[...] = zrow[...].astype(F32)
    table = zrow32[:, 16:32, :].reshape(ZS * 16, 128).astype(BF)
    wanted = jnp.sum(jnp.where(here, nn(spread, table), 0.0), axis=1, keepdims=True)
    tall = lax.broadcasted_iota(jnp.int32, (256, 64), 0)
    node = lax.broadcasted_iota(jnp.int32, (256, 64), 1)
    chosen = ((node >> 3) == (tall & 7)) & ((node & 7).astype(F32) == wanted)
    pick_s[...] = chosen.astype(F32).astype(BF)
    for k in range(2):
        rows = zrow32[:, 8 * k : 8 * k + 8, :].reshape(64, 128).astype(BF)
        psel[:, :, 128 * k : 128 * k + 128] = nn(pick_s[...], rows).astype(BF).reshape(8, 32, 128)
    p_rows = [remote(psel.at[m], prow.at[m], pg_sem, m - 1, nodes=plane(m, 1)) for m in (4, 5, 2, 3, 6, 7, 1)]
    for copy in p_rows:
        copy.start()
    prow[0] = psel[0]
    for copy in z_raws:
        copy.wait()
    zraw32[...] = zraw[...].astype(F32)
    for i in range(4):
        rows = zraw32[:, 8 * i : 8 * i + 8, :].reshape(64, 128).astype(BF)
        praw_s[:, :, 128 * i : 128 * i + 128] = nn(pick_s[...], rows).astype(BF).reshape(8, 32, 128)
    p_raws = [
        remote(praw_s.at[m], praw_r.at[m], pr_sem, m - 1, nodes=plane(m, 1)) for m in (4, 5, 2, 3, 6, 7, 1)
    ]
    for copy in p_raws:
        copy.start()
    praw_r[0] = praw_s[0]
    pick_t[...] = nt(eye(64), pick_s[...]).astype(BF)

    for copy in halos:
        copy.wait()
    row = lax.broadcasted_iota(jnp.int32, (2 * HALO, D), 0)
    outside = ((row < HALO) & (b == 0)) | ((row >= HALO) & (b == NODES - 1))
    rim = jnp.where(outside, 0.0, halo[...].astype(F32)).astype(BF)
    for k in range(2):
        latt[256 * k : 256 * k + 256, ROWS : ROWS + 2 * HALO] = nt(eye256, rim[:, 256 * k : 256 * k + 256]).astype(BF)
    hi, lo = split(nn(wst[...], latt[:, ROWS : ROWS + 2 * HALO]))
    a_src[0:H, ROWS : ROWS + 2 * HALO] = hi
    a_src[H : 2 * H, ROWS : ROWS + 2 * HALO] = lo

    def edges(k, from_s, live_row):
        pre = pre_in[k] + from_s
        sig = 0.5 + 0.5 * jnp.tanh(0.5 * pre)
        act = pre * sig
        slope = sig + act * (1.0 - sig)
        return (back_in[k] * slope).astype(BF), (act * live_row.astype(F32)).astype(BF)

    for k in range(FINE // CH):
        at = slice(k * CH, (k + 1) * CH)
        from_s = nn(a_src[:, ROWS : ROWS + 2 * HALO], oh_s[k, ROWS : ROWS + 2 * HALO, :])
        grad, hidden = edges(k, from_s[0:H] + from_s[H : 2 * H], fv[at].reshape(1, CH))
        add_s, add_r = nt(oh_s[k], grad), nt(oh_r[k], jnp.concatenate([grad, hidden], 0))
        if k == 0:
            g_src[...] = add_s
            g_rh[...] = add_r
        else:
            g_src[...] += add_s
            g_rh[...] += add_r

    rim_s[...] = g_src[ROWS : ROWS + 2 * HALO, :].astype(BF)
    rims = (
        remote(rim_s.at[0:HALO], rim_r.at[HALO : 2 * HALO], rim_sem, 0, nodes=down),
        remote(rim_s.at[HALO : 2 * HALO], rim_r.at[0:HALO], rim_sem, 1, nodes=up),
    )
    for copy in rims:
        copy.start()

    for copy in p_rows:
        copy.wait()
    a_slot[...] = nt(eye256, prow[...].reshape(256, H)).astype(BF)
    grad, hidden = edges(3, nn(a_slot[...], oh_c[...]), cv[...])

    bufs, rcs, xss, rxs = (buf0, buf1, buf2), (rc0, rc1, rc2), (xs0, xs1, xs2), (rx0, rx1, rx2)
    zss, rzs = (zs0, zs1, zs2), (rz0, rz1, rz2)

    def lay_out(buf, value):
        for d in range(NODES):
            piece = value[8 * d : 8 * d + 8, :]
            tile = jnp.concatenate([piece[:, 0:128], piece[:, 128:256]], 0)
            buf[d % 2, (d // 2) % XS, d // (2 * XS)] = tile.astype(BF)

    cores = []

    def send_core(a):
        copy = remote(bufs[a].at[1 - c], rcs[a], core_sem, a, nodes=b + 1 - 2 * c)
        copy.start()
        cores.append(copy)

    x_copies = []

    def send_x(a):
        cores[a].wait()
        xss[a][...] = (bufs[a][c].astype(F32) + rcs[a][...].astype(F32)).astype(BF)
        for k in (2, 1, 3):
            to = lax.rem(x + k, XS)
            copy = remote(
                xss[a].at[to], rxs[a].at[k - 1], x_sem, 3 * a + k - 1, nodes=(z * XS + to) * 2 + c
            )
            copy.start()
            x_copies.append(copy)

    g_slot[...] = nt(oh_c[...], grad).astype(BF)
    ret_s[...] = g_slot[...].reshape(8, 32, H)
    backs = [remote(ret_s.at[m], ret_r.at[m], rp_sem, m - 1, nodes=plane(m, -1)) for m in (4, 5, 2, 3, 6, 7, 1)]
    for copy in backs:
        copy.start()
    ret_r[0] = ret_s[0]

    lay_out(buf0, nn(cott[...], (g_rh[:, H : 2 * H] + nt(oh_r[3], hidden)).astype(BF)))
    send_core(0)

    g_recv = g_rh[:, 0:H] + nt(oh_r[3], grad)
    lay_out(buf1, nn(latt[:, 0:ROWS], g_recv.astype(BF)))
    total = jnp.sum(g_recv, axis=0, keepdims=True)
    bias_tile = jnp.concatenate([total[:, 0:128], total[:, 128:256], jnp.zeros((14, 128), F32)], 0).astype(BF)
    for i in range(2):
        for k in range(XS):
            buf1[i, k, 8] = bias_tile
    send_core(1)
    send_x(0)
    for copy in p_raws:
        copy.wait()
    arr = praw_r[...].reshape(256, D)
    for k in range(2):
        latt[256 * k : 256 * k + 256, 384:640] = nt(eye256, arr[:, 256 * k : 256 * k + 256]).astype(BF)
    lay_out(
        buf2,
        nn(latt[:, 0 : ROWS + 2 * HALO], g_src[...].astype(BF)) + nn(latt[:, 384:640], g_slot[...]),
    )
    send_core(2)
    send_x(1)

    for copy in rims:
        copy.wait()
    low_rows = g_src[0:HALO, :]
    low = jnp.where(b == 0, 0.0, rim_r[0:HALO, :].astype(F32))
    high = jnp.where(b == NODES - 1, 0.0, rim_r[HALO : 2 * HALO, :].astype(F32))
    sent = jnp.concatenate(
        [low_rows + low, g_src[HALO : ROWS - HALO, :], g_src[ROWS - HALO : ROWS, :] + high], 0
    )
    node = nt(ws[...], sent.astype(BF)) + nt(wr[...], g_recv.astype(BF))
    part[...] = node.reshape(HID, 64, ROWS)
    ys[...] = node.astype(BF).reshape(HID, 64, ROWS)
    y_copies = []
    for k in (4, 3, 5, 2, 6, 1, 7):
        to = lax.rem(y + k, HID)
        copy = remote(ys.at[to], ry.at[k - 1], y_sem, k - 1, hid=to)
        copy.start()
        y_copies.append(copy)

    send_x(2)

    for copy in backs:
        copy.wait()
    summed = nn(pick_t[...], ret_r[...].reshape(256, H)).reshape(ZS, 8, H)
    for k in range(ZS):
        col_s[k] = jnp.concatenate([summed[k, :, 0:128], summed[k, :, 128:256]], 0).astype(BF)
    cols = [remote(col_s.at[k], col_r.at[k], rz_sem, k - 1, nodes=column(k, -1)) for k in (4, 3, 5, 2, 6, 1, 7)]
    for copy in cols:
        copy.start()
    col_r[0] = col_s[0]

    z_copies = []
    for a in range(3):
        for copy in x_copies[3 * a : 3 * a + 3]:
            copy.wait()
        mine = bufs[a][c, x].astype(F32) + rcs[a][x].astype(F32)
        for k in range(3):
            mine += rxs[a][k].astype(F32)
        sums[0:8] = mine[0:8]
        own[a] = sums[z]
        zss[a][:, 0:16, :] = mine[0:8].astype(BF)
        if a == 1:
            own[3] = mine[8]
            for k in range(ZS):
                zss[a][k, 16:32, :] = mine[8].astype(BF)
        for k in (4, 3, 5, 2, 6, 1, 7):
            to = lax.rem(z + k, ZS)
            copy = remote(
                zss[a].at[to], rzs[a].at[k - 1], z_sem, 7 * a + k - 1, nodes=(to * XS + x) * 2 + c
            )
            copy.start()
            z_copies.append(copy)

    own_out = pltpu.make_async_copy(own, own_h, out_sem.at[0])
    own_out.start()

    for copy in cols:
        copy.wait()
    tile = col_r[0].astype(F32)
    for k in range(1, ZS):
        tile += col_r[k].astype(F32)
    coarse = jnp.concatenate([tile[0:8], tile[8:16]], 1)
    coarse = jnp.concatenate([coarse, jnp.zeros((8, H), F32)], 0)
    hi, lo = split(coarse)
    coarse_part = nt(hi, ws[...]) + nt(lo, ws[...])
    for k in range(HID):
        cy[k] = coarse_part[0:8, 128 * (k // 2) : 128 * (k // 2) + 128]
    cy_copies = []
    for k in (4, 3, 5, 2, 6, 1, 7):
        to = lax.rem(y + k, HID)
        copy = remote(cy.at[to], rcy.at[k - 1], cy_sem, k - 1, hid=to)
        copy.start()
        cy_copies.append(copy)

    cy_out = pltpu.make_async_copy(cy.at[y], rcy.at[HID - 1], out_sem.at[1])
    cy_out.start()

    for copy in y_copies:
        copy.wait()
    mine = part[y] + cott[pl.ds(pl.multiple_of(y * 64, 64), 64), :].astype(F32)
    for k in range(HID - 1):
        mine += ry[k].astype(F32)
    node_v[...] = mine
    node_out = pltpu.make_async_copy(node_v, node_h, out_sem.at[2])
    node_out.start()

    for copy in z_copies + cy_copies + [own_out, cy_out, node_out]:
        copy.wait()


def finish(
    rz0_h, rz1_h, rz2_h, own_h, node_h, rcy_h,
    n_out, s_out, r_out, o_out, b_out,
    rz0, rz1, rz2, own, node, rcy, n_v, s_v, r_v, o_v, b_v, in_sem, out_sem,
):
    b = lax.axis_index("nodes")
    y = lax.axis_index("hid")
    reads = [
        pltpu.make_async_copy(src, dst, in_sem.at[i])
        for i, (src, dst) in enumerate(
            ((own_h, own), (rz0_h, rz0), (rz1_h, rz1), (rz2_h, rz2), (rcy_h, rcy), (node_h, node))
        )
    ]
    for copy in reads:
        copy.start()
    writes = []

    def write(i, src, dst):
        copy = pltpu.make_async_copy(src, dst, out_sem.at[i])
        copy.start()
        writes.append(copy)

    reads[0].wait()
    for a, (rz, vec, out) in enumerate(((rz0, o_v, o_out), (rz1, r_v, r_out), (rz2, s_v, s_out))):
        reads[1 + a].wait()
        tile = own[a]
        for k in range(ZS - 1):
            tile += rz[k, 0:16].astype(F32)
        vec[...] = jnp.concatenate([tile[0:8], tile[8:16]], 1)
        write(a, vec, out)
    tile = own[3]
    for k in range(ZS - 1):
        tile += rz1[k, 16:32].astype(F32)
    line = jnp.broadcast_to(jnp.where(b < NODES // 2, tile[0:1], tile[1:2]), (8, 128))
    lane = lax.broadcasted_iota(jnp.int32, (128, 128), 0)
    want = lax.broadcasted_iota(jnp.int32, (128, 128), 1) + 4 * lax.rem(b, NODES // 2)
    take = (lane == want).astype(F32).astype(BF)
    v0 = line.astype(BF)
    rest = line - v0.astype(F32)
    v1 = rest.astype(BF)
    v2 = (rest - v1.astype(F32)).astype(BF)
    b_v[...] = (nn(v0, take) + nn(v1, take) + nn(v2, take))[0, 0:4]
    write(4, b_v, b_out)

    reads[4].wait()
    late = rcy[HID - 1]
    for k in range(HID - 1):
        late += rcy[k]
    late = jnp.concatenate([late, jnp.zeros((120, 128), F32)], 0).T
    late = jnp.where(lax.rem(y, 2) == 0, late[0:64, :], late[64:128, :])
    reads[5].wait()
    n_v[:, 0:128] = node[:, 0:128] + late
    n_v[:, 128:256] = node[:, 128:256]
    write(3, n_v, n_out)
    for copy in writes:
        copy.wait()


def vm(shape, dtype):
    return pltpu.VMEM(shape, dtype)


def shards(
    latents, cotangent, w_send, w_recv, bias, w_out, fine_sender, fine_receiver, fine_valid,
    send_rows, coarse_slot, coarse_receiver, coarse_valid,
):
    i32 = jnp.int32
    operands = (
        latents, cotangent, w_send, w_recv, bias.reshape(1, H), w_out,
        fine_sender, fine_receiver, fine_valid,
        send_rows[0].T,
        coarse_slot.reshape(1, COARSE), coarse_receiver.reshape(1, COARSE), coarse_valid.reshape(1, COARSE),
    )
    sems = pltpu.SemaphoreType.DMA
    scratch = [vm((16, D), BF)] + [vm(v.shape, v.dtype) for v in operands] + [sems((14,))]
    scratch += [
        vm((32, 128), F32), vm((ZS, 32, 128), BF), vm((ZS, 32, 128), F32), vm((ZS, 32, 128), BF),
        vm((ZS, 32, 128), F32), vm((256, 64), BF), vm((64, 256), BF),
        vm((8, 32, H), BF), vm((8, 32, H), BF), vm((8, 32, D), BF), vm((8, 32, D), BF),
        vm((2 * HALO, D), BF), vm((H, D), BF), vm((D, 640), BF), vm((D, ROWS), BF),
        vm((2 * H, 384), BF), vm((3 * H, ROWS), BF), vm((H, 256), BF),
        vm((3, 384, CH), BF), vm((4, ROWS, CH), BF), vm((256, CH), BF), vm((4, H, CH), F32), vm((4, H, CH), F32),
        vm((384, H), F32), vm((ROWS, 2 * H), F32), vm((256, H), BF),
        vm((8, 32, H), BF), vm((8, 32, H), BF), vm((ZS, 16, 128), BF), vm((ZS, 16, 128), BF),
        vm((2 * HALO, H), BF), vm((2 * HALO, H), BF),
    ]
    scratch += [vm((2, XS, t, 16, 128), BF) for t in TILES]
    scratch += [vm((XS, t, 16, 128), BF) for t in TILES]
    scratch += [vm((XS, t, 16, 128), BF) for t in TILES]
    scratch += [vm((XS - 1, t, 16, 128), BF) for t in TILES]
    scratch += [vm((ZS, 16, 128), F32), vm((4, 16, 128), F32)]
    scratch += [vm((ZS, 16 * (t - 7), 128), BF) for t in TILES]
    scratch += [
        vm((HID, 64, ROWS), F32), vm((HID, 64, ROWS), BF), vm((HID - 1, 64, ROWS), BF),
        vm((64, ROWS), F32), vm((HID, 8, 128), F32),
    ]
    scratch += [
        sems((2, 7)), sems((2, 7)), sems((2, 7)), sems((2, 7)), sems((2, 2)), sems((2, 7)), sems((2, 7)), sems((2, 2)), sems((2, 3)), sems((2, 9)), sems((2, 21)),
        sems((2, 7)), sems((2, 7)), sems((3,)),
    ]
    hbm = pl.BlockSpec(memory_space=pltpu.MemorySpace.HBM)
    kept = [
        ((ZS - 1, 16, 128), BF), ((ZS - 1, 32, 128), BF), ((ZS - 1, 16, 128), BF),
        ((4, 16, 128), F32), ((64, ROWS), F32), ((HID, 8, 128), F32),
    ]
    arrived = pl.pallas_call(
        kernel,
        out_shape=[jax.ShapeDtypeStruct(shape, dtype) for shape, dtype in kept],
        in_specs=[hbm] * 13,
        out_specs=[hbm] * 6,
        scratch_shapes=scratch,
        compiler_params=pltpu.CompilerParams(
            collective_id=0, has_side_effects=True, vmem_limit_bytes=64 * 1024 * 1024
        ),
        name="edge_update",
    )(*operands)
    results = [(64, ROWS), (8, H), (8, H), (8, H)]
    out_n, out_s, out_r, out_o, out_b = pl.pallas_call(
        finish,
        out_shape=[jax.ShapeDtypeStruct(shape, F32) for shape in results + [(4,)]],
        in_specs=[hbm] * 6,
        out_specs=[hbm] * 5,
        scratch_shapes=[vm(shape, dtype) for shape, dtype in kept]
        + [vm(shape, F32) for shape in results + [(4,)]]
        + [sems((6,)), sems((5,))],
        compiler_params=pltpu.CompilerParams(vmem_limit_bytes=64 * 1024 * 1024),
        name="finish",
    )(*arrived)
    return out_n.T, out_s, out_r, out_o.T, out_b


def solution(mesh):
    return jax.shard_map(
        shards,
        mesh=mesh,
        in_specs=(
            P("nodes", None), P("nodes", None), P(None, "hid"), P(None, "hid"), P("hid"), P("hid", None),
            P("nodes"), P("nodes"), P("nodes"), P("nodes", None, None), P("nodes"), P("nodes"), P("nodes"),
        ),
        out_specs=(
            P("nodes", "hid"), P("nodes", "hid"), P("nodes", "hid"), P("hid", "nodes"), P(("hid", "nodes")),
        ),
        check_vma=False,
    )
```

```python
import jax
import jax.numpy as jnp
from jax import lax
from jax.experimental import pallas as pl
from jax.experimental.pallas import tpu as pltpu
from jax.sharding import PartitionSpec as P

BF = jnp.bfloat16
F32 = jnp.float32
MESH = pl.DeviceIdType.MESH
NODES = 64
HID = 8
ZS, XS = 8, 4
ROWS = 256
D = 512
H = 256
HALO = 64
FINE = 1536
COARSE = 512
CH = 512
TILES = (8, 9, 8)


def nn(a, b):
    return lax.dot_general(a, b, (((1,), (0,)), ((), ())), preferred_element_type=F32)


def nt(a, b):
    return lax.dot_general(a, b, (((1,), (1,)), ((), ())), preferred_element_type=F32)


def split(v):
    hi = v.astype(BF)
    return hi, (v - hi.astype(F32)).astype(BF)


def one_hot(count, row):
    return (lax.broadcasted_iota(jnp.int32, (count, row.shape[1]), 0) == row).astype(F32).astype(BF)


def eye(n):
    a = lax.broadcasted_iota(jnp.int32, (n, n), 0)
    b = lax.broadcasted_iota(jnp.int32, (n, n), 1)
    return (a == b).astype(F32).astype(BF)


def kernel(
    lat_h, cot_h, ws_h, wr_h, bias_h, wo_h, fs_h, fr_h, fv_h, sr_h, cs_h, cr_h, cv_h,
    rz0, rz1, rz2, own_h, node_h, rcy,
    low, lat, cot, ws, wr, bias, wo, fs, fr, fv, sr, cs, cr, cv, load_sem,
    msg32, zrow, zrow32, zraw, zraw32, pick_s, pick_t, psel, prow, praw_s, praw_r, halo, wst, latt, cott, a_src, a_rcv, a_slot, oh_s, oh_r, oh_c, pre_in, back_in,
    g_src, g_rh, g_slot,
    ret_s, ret_r, col_s, col_r, rim_s, rim_r,
    buf0, buf1, buf2, rc0, rc1, rc2, xs0, xs1, xs2, rx0, rx1, rx2, sums, own, zs0, zs1, zs2,
    part, ys, ry, node_v, cy,
    zg_sem, pg_sem, zr_sem, pr_sem, halo_sem, rp_sem, rz_sem, rim_sem, core_sem, x_sem, z_sem, y_sem, cy_sem, out_sem,
):
    b = lax.axis_index("nodes")
    y = lax.axis_index("hid")
    c = lax.rem(b, 2)
    x = lax.rem(b // 2, XS)
    z = b // (2 * XS)
    bar = pltpu.get_barrier_semaphore()

    loads = [
        pltpu.make_async_copy(src, dst, load_sem.at[i])
        for i, (src, dst) in enumerate(
            (
                (sr_h, sr), (ws_h, ws), (lat_h, lat), (wr_h, wr), (cot_h, cot), (wo_h, wo), (bias_h, bias),
                (fs_h, fs), (fr_h, fr), (fv_h, fv), (cs_h, cs), (cr_h, cr), (cv_h, cv),
            )
        )
    ]
    first = pltpu.make_async_copy(lat_h.at[0:16], low, load_sem.at[13])
    first.start()
    for load in loads[0:2]:
        load.start()

    def block(zz, xx, cc):
        return (zz * XS + xx) * 2 + cc

    def plane(m, sign):
        return block(z, lax.rem(x + XS + sign * (m // 2), XS), lax.rem(c + m % 2, 2))

    def column(k, sign):
        return block(lax.rem(z + ZS + sign * k, ZS), x, c)

    def greet(**device):
        pl.semaphore_signal(bar, inc=1, device_id=device, device_id_type=MESH)

    for k in (4, 3, 5):
        greet(nodes=column(k, 1))
        greet(hid=lax.rem(y + k, HID))
    for m in (5, 4, 3, 2, 7, 6, 1):
        greet(nodes=plane(m, 1))
    for k in (2, 6, 1, 7):
        greet(nodes=column(k, 1))
        greet(hid=lax.rem(y + k, HID))
    greet(nodes=lax.rem(b + NODES - 1 + 2 * c, NODES))
    for load in loads[2:]:
        load.start()

    def remote(src, dst, sems, at, **device):
        return pltpu.make_async_remote_copy(
            src_ref=src, dst_ref=dst, send_sem=sems.at[0, at], recv_sem=sems.at[1, at],
            device_id=device, device_id_type=MESH,
        )

    msg32[...] = jnp.zeros_like(msg32)
    loads[0].wait()
    msg32[16:20, 0:NODES] = sr[...].astype(F32)
    first.wait()
    low32 = low[...].astype(F32)
    for k in range(4):
        zraw32[0, 8 * k : 8 * k + 8, :] = low32[0:8, 128 * k : 128 * k + 128]
    zraw[0] = zraw32[0].astype(BF)
    loads[1].wait()
    ahead = nn(low[...], ws[...])
    for k in range(2):
        msg32[8 * k : 8 * k + 8, :] = ahead[0:8, 128 * k : 128 * k + 128]
    zrow[0] = msg32[...].astype(BF)

    pl.semaphore_wait(bar, 22)

    z_rows = [remote(zrow.at[0], zrow.at[k], zg_sem, k - 1, nodes=column(k, 1)) for k in (4, 3, 5, 2, 6, 1, 7)]
    for copy in z_rows:
        copy.start()
    z_raws = [remote(zraw.at[0], zraw.at[k], zr_sem, k - 1, nodes=column(k, 1)) for k in (4, 3, 5, 2, 6, 1, 7)]
    for copy in z_raws:
        copy.start()
    loads[2].wait()
    up = lax.rem(b + 1, NODES)
    down = lax.rem(b + NODES - 1, NODES)
    halos = (
        remote(lat.at[ROWS - HALO : ROWS], halo.at[0:HALO], halo_sem, 0, nodes=up),
        remote(lat.at[0:HALO], halo.at[HALO : 2 * HALO], halo_sem, 1, nodes=down),
    )
    for copy in halos:
        copy.start()


    for load in loads[3:]:
        load.wait()
    eye256 = eye(256)
    wst[...] = nt(eye256, ws[...]).astype(BF)
    wrt = nt(eye256, wr[...]).astype(BF)
    bias_row = bias[...]
    b0 = bias_row.astype(BF)
    rest = bias_row - b0.astype(F32)
    b1 = rest.astype(BF)
    b2 = (rest - b1.astype(F32)).astype(BF)
    b_rows = jnp.concatenate([b0.astype(F32), b1.astype(F32), b2.astype(F32), jnp.zeros((5, H), F32)], 0)
    bias_col = jnp.sum(nt(eye256, b_rows.astype(BF)), axis=1, keepdims=True)
    for k in range(2):
        latt[256 * k : 256 * k + 256, 0:ROWS] = nt(eye256, lat[:, 256 * k : 256 * k + 256]).astype(BF)
        cott[256 * k : 256 * k + 256, :] = nt(eye256, cot[:, 256 * k : 256 * k + 256]).astype(BF)
    hi, lo = split(nn(wst[...], latt[:, 0:ROWS]))
    a_src[0:H, 0:ROWS] = hi
    a_src[H : 2 * H, 0:ROWS] = lo
    hi, lo = split(nn(wrt, latt[:, 0:ROWS]) + bias_col)
    a_rcv[0:H, :] = hi
    a_rcv[H : 2 * H, :] = lo
    a_rcv[2 * H : 3 * H, :] = nt(wo[...], cot[...]).astype(BF)

    for k in range(4):
        at = slice(k * CH, (k + 1) * CH)
        ends, live = (fr[at], fv[at]) if k < 3 else (cr[0, :], cv[0, :])
        oh_r[k] = one_hot(ROWS, ends.reshape(1, CH))
        from_r = nn(a_rcv[...], oh_r[k])
        back_in[k] = from_r[2 * H :] * live.reshape(1, CH).astype(F32)
        pre = from_r[0:H] + from_r[H : 2 * H]
        if k < 3:
            s = fs[at].reshape(1, CH)
            s = jnp.where(s < HALO, s + ROWS, jnp.where(s < HALO + ROWS, s - HALO, s))
            oh_s[k] = one_hot(ROWS + 2 * HALO, s)
            from_s = nn(a_src[:, 0:ROWS], oh_s[k, 0:ROWS, :])
            pre += from_s[0:H] + from_s[H : 2 * H]
        pre_in[k] = pre

    wide = lax.broadcasted_iota(jnp.int32, (256, 128), 0)
    lane = lax.broadcasted_iota(jnp.int32, (256, 128), 1)
    spread = (lane == (wide & 7) * 16 + ((wide >> 3) & 3)).astype(F32).astype(BF)
    asked = ((z * XS + ((x + (wide >> 6)) & (XS - 1))) << 1) + ((c + (wide >> 5)) & 1)
    here = lane == asked
    q = cs[...]
    place = (
        (((x + XS - ((q >> 3) & (XS - 1))) & (XS - 1)) << 6)
        + (((c + (q >> 2)) & 1) << 5)
        + ((q & 3) << 3)
        + ((z + ZS - (q >> 5)) & (ZS - 1))
    )
    oh_c[...] = one_hot(256, place)

    for copy in z_rows:
        copy.wait()
    zrow32[...] = zrow[...].astype(F32)
    table = zrow32[:, 16:32, :].reshape(ZS * 16, 128).astype(BF)
    wanted = jnp.sum(jnp.where(here, nn(spread, table), 0.0), axis=1, keepdims=True)
    tall = lax.broadcasted_iota(jnp.int32, (256, 64), 0)
    node = lax.broadcasted_iota(jnp.int32, (256, 64), 1)
    chosen = ((node >> 3) == (tall & 7)) & ((node & 7).astype(F32) == wanted)
    pick_s[...] = chosen.astype(F32).astype(BF)
    for k in range(2):
        rows = zrow32[:, 8 * k : 8 * k + 8, :].reshape(64, 128).astype(BF)
        psel[:, :, 128 * k : 128 * k + 128] = nn(pick_s[...], rows).astype(BF).reshape(8, 32, 128)
    p_rows = [remote(psel.at[m], prow.at[m], pg_sem, m - 1, nodes=plane(m, 1)) for m in (5, 4, 3, 2, 7, 6, 1)]
    for copy in p_rows:
        copy.start()
    prow[0] = psel[0]
    for copy in z_raws:
        copy.wait()
    zraw32[...] = zraw[...].astype(F32)
    for i in range(4):
        rows = zraw32[:, 8 * i : 8 * i + 8, :].reshape(64, 128).astype(BF)
        praw_s[:, :, 128 * i : 128 * i + 128] = nn(pick_s[...], rows).astype(BF).reshape(8, 32, 128)
    p_raws = [
        remote(praw_s.at[m], praw_r.at[m], pr_sem, m - 1, nodes=plane(m, 1)) for m in (5, 4, 3, 2, 7, 6, 1)
    ]
    for copy in p_raws:
        copy.start()
    praw_r[0] = praw_s[0]
    pick_t[...] = nt(eye(64), pick_s[...]).astype(BF)

    for copy in halos:
        copy.wait()
    row = lax.broadcasted_iota(jnp.int32, (2 * HALO, D), 0)
    outside = ((row < HALO) & (b == 0)) | ((row >= HALO) & (b == NODES - 1))
    rim = jnp.where(outside, 0.0, halo[...].astype(F32)).astype(BF)
    for k in range(2):
        latt[256 * k : 256 * k + 256, ROWS : ROWS + 2 * HALO] = nt(eye256, rim[:, 256 * k : 256 * k + 256]).astype(BF)
    hi, lo = split(nn(wst[...], latt[:, ROWS : ROWS + 2 * HALO]))
    a_src[0:H, ROWS : ROWS + 2 * HALO] = hi
    a_src[H : 2 * H, ROWS : ROWS + 2 * HALO] = lo

    def edges(k, from_s, live_row, at=slice(0, CH)):
        pre = pre_in[k, :, at] + from_s
        sig = 0.5 + 0.5 * jnp.tanh(0.5 * pre)
        act = pre * sig
        slope = sig + act * (1.0 - sig)
        return (back_in[k, :, at] * slope).astype(BF), (act * live_row.astype(F32)).astype(BF)

    for k in range(FINE // CH):
        at = slice(k * CH, (k + 1) * CH)
        from_s = nn(a_src[:, ROWS : ROWS + 2 * HALO], oh_s[k, ROWS : ROWS + 2 * HALO, :])
        grad, hidden = edges(k, from_s[0:H] + from_s[H : 2 * H], fv[at].reshape(1, CH))
        add_s, add_r = nt(oh_s[k], grad), nt(oh_r[k], jnp.concatenate([grad, hidden], 0))
        if k == 0:
            g_src[...] = add_s
            g_rh[...] = add_r
        else:
            g_src[...] += add_s
            g_rh[...] += add_r

    rim_s[...] = g_src[ROWS : ROWS + 2 * HALO, :].astype(BF)
    rims = (
        remote(rim_s.at[0:HALO], rim_r.at[HALO : 2 * HALO], rim_sem, 0, nodes=down),
        remote(rim_s.at[HALO : 2 * HALO], rim_r.at[0:HALO], rim_sem, 1, nodes=up),
    )
    for copy in rims:
        copy.start()

    for copy in p_rows:
        copy.wait()
    a_slot[...] = nt(eye256, prow[...].reshape(256, H)).astype(BF)
    halves = []
    for k in range(2):
        at = slice(k * CH // 2, (k + 1) * CH // 2)
        halves.append(edges(3, nn(a_slot[...], oh_c[:, at]), cv[:, at], at))
    grad = jnp.concatenate([half[0] for half in halves], 1)
    hidden = jnp.concatenate([half[1] for half in halves], 1)

    bufs, rcs, xss, rxs = (buf0, buf1, buf2), (rc0, rc1, rc2), (xs0, xs1, xs2), (rx0, rx1, rx2)
    zss, rzs = (zs0, zs1, zs2), (rz0, rz1, rz2)

    def lay_out(buf, value):
        for d in range(NODES):
            piece = value[8 * d : 8 * d + 8, :]
            tile = jnp.concatenate([piece[:, 0:128], piece[:, 128:256]], 0)
            buf[d % 2, (d // 2) % XS, d // (2 * XS)] = tile.astype(BF)

    cores = []

    def send_core(a):
        copy = remote(bufs[a].at[1 - c], rcs[a], core_sem, a, nodes=b + 1 - 2 * c)
        copy.start()
        cores.append(copy)

    x_copies = []

    def send_x(a):
        cores[a].wait()
        for k in (2, 1, 3):
            to = lax.rem(x + k, XS)
            xss[a][to] = (bufs[a][c, to].astype(F32) + rcs[a][to].astype(F32)).astype(BF)
            copy = remote(
                xss[a].at[to], rxs[a].at[k - 1], x_sem, 3 * a + k - 1, nodes=(z * XS + to) * 2 + c
            )
            copy.start()
            x_copies.append(copy)

    g_slot[...] = nt(oh_c[...], grad).astype(BF)
    ret_s[...] = g_slot[...].reshape(8, 32, H)
    backs = [remote(ret_s.at[m], ret_r.at[m], rp_sem, m - 1, nodes=plane(m, -1)) for m in (5, 4, 3, 2, 7, 6, 1)]
    for copy in backs:
        copy.start()
    ret_r[0] = ret_s[0]

    lay_out(buf0, nn(cott[...], (g_rh[:, H : 2 * H] + nt(oh_r[3], hidden)).astype(BF)))
    send_core(0)

    g_recv = g_rh[:, 0:H] + nt(oh_r[3], grad)
    lay_out(buf1, nn(latt[:, 0:ROWS], g_recv.astype(BF)))
    total = jnp.sum(g_recv, axis=0, keepdims=True)
    bias_tile = jnp.concatenate([total[:, 0:128], total[:, 128:256], jnp.zeros((14, 128), F32)], 0).astype(BF)
    for i in range(2):
        for k in range(XS):
            buf1[i, k, 8] = bias_tile
    send_core(1)
    send_x(0)
    for copy in p_raws:
        copy.wait()
    arr = praw_r[...].reshape(256, D)
    for k in range(2):
        latt[256 * k : 256 * k + 256, 384:640] = nt(eye256, arr[:, 256 * k : 256 * k + 256]).astype(BF)
    lay_out(
        buf2,
        nn(latt[:, 0 : ROWS + 2 * HALO], g_src[...].astype(BF)) + nn(latt[:, 384:640], g_slot[...]),
    )
    send_core(2)
    send_x(1)

    for copy in rims:
        copy.wait()
    low_rows = g_src[0:HALO, :]
    low = jnp.where(b == 0, 0.0, rim_r[0:HALO, :].astype(F32))
    high = jnp.where(b == NODES - 1, 0.0, rim_r[HALO : 2 * HALO, :].astype(F32))
    sent = jnp.concatenate(
        [low_rows + low, g_src[HALO : ROWS - HALO, :], g_src[ROWS - HALO : ROWS, :] + high], 0
    )
    node = nt(ws[...], sent.astype(BF)) + nt(wr[...], g_recv.astype(BF))
    part[...] = node.reshape(HID, 64, ROWS)
    ys[...] = node.astype(BF).reshape(HID, 64, ROWS)
    y_copies = []
    for k in (4, 3, 5, 2, 6, 1, 7):
        to = lax.rem(y + k, HID)
        copy = remote(ys.at[to], ry.at[k - 1], y_sem, k - 1, hid=to)
        copy.start()
        y_copies.append(copy)

    send_x(2)

    for copy in backs:
        copy.wait()
    summed = nn(pick_t[...], ret_r[...].reshape(256, H)).reshape(ZS, 8, H)
    for k in range(ZS):
        col_s[k] = jnp.concatenate([summed[k, :, 0:128], summed[k, :, 128:256]], 0).astype(BF)
    cols = [remote(col_s.at[k], col_r.at[k], rz_sem, k - 1, nodes=column(k, -1)) for k in (4, 3, 5, 2, 6, 1, 7)]
    for copy in cols:
        copy.start()
    col_r[0] = col_s[0]

    z_copies = []
    for a in range(3):
        for copy in x_copies[3 * a : 3 * a + 3]:
            copy.wait()
        mine = bufs[a][c, x].astype(F32) + rcs[a][x].astype(F32)
        for k in range(3):
            mine += rxs[a][k].astype(F32)
        sums[0:8] = mine[0:8]
        own[a] = sums[z]
        zss[a][:, 0:16, :] = mine[0:8].astype(BF)
        if a == 1:
            own[3] = mine[8]
            for k in range(ZS):
                zss[a][k, 16:32, :] = mine[8].astype(BF)
        for k in (4, 3, 5, 2, 6, 1, 7):
            to = lax.rem(z + k, ZS)
            copy = remote(
                zss[a].at[to], rzs[a].at[k - 1], z_sem, 7 * a + k - 1, nodes=(to * XS + x) * 2 + c
            )
            copy.start()
            z_copies.append(copy)

    own_out = pltpu.make_async_copy(own, own_h, out_sem.at[0])
    own_out.start()

    for copy in cols:
        copy.wait()
    tile = col_r[0].astype(F32)
    for k in range(1, ZS):
        tile += col_r[k].astype(F32)
    coarse = jnp.concatenate([tile[0:8], tile[8:16]], 1)
    coarse = jnp.concatenate([coarse, jnp.zeros((8, H), F32)], 0)
    hi, lo = split(coarse)
    coarse_part = nt(hi, ws[...]) + nt(lo, ws[...])
    for k in range(HID):
        cy[k] = coarse_part[0:8, 128 * (k // 2) : 128 * (k // 2) + 128]
    cy_copies = []
    for k in (4, 3, 5, 2, 6, 1, 7):
        to = lax.rem(y + k, HID)
        copy = remote(cy.at[to], rcy.at[k - 1], cy_sem, k - 1, hid=to)
        copy.start()
        cy_copies.append(copy)

    cy_out = pltpu.make_async_copy(cy.at[y], rcy.at[HID - 1], out_sem.at[1])
    cy_out.start()

    for copy in y_copies:
        copy.wait()
    mine = part[y] + cott[pl.ds(pl.multiple_of(y * 64, 64), 64), :].astype(F32)
    for k in range(HID - 1):
        mine += ry[k].astype(F32)
    node_v[...] = mine
    node_out = pltpu.make_async_copy(node_v, node_h, out_sem.at[2])
    node_out.start()

    for copy in z_copies + cy_copies + [own_out, cy_out, node_out]:
        copy.wait()


def finish(
    rz0_h, rz1_h, rz2_h, own_h, node_h, rcy_h,
    n_out, s_out, r_out, o_out, b_out,
    rz0, rz1, rz2, own, node, rcy, n_v, s_v, r_v, o_v, b_v, in_sem, out_sem,
):
    b = lax.axis_index("nodes")
    y = lax.axis_index("hid")
    reads = [
        pltpu.make_async_copy(src, dst, in_sem.at[i])
        for i, (src, dst) in enumerate(
            ((own_h, own), (rz0_h, rz0), (rz1_h, rz1), (rz2_h, rz2), (rcy_h, rcy), (node_h, node))
        )
    ]
    for copy in reads:
        copy.start()
    writes = []

    def write(i, src, dst):
        copy = pltpu.make_async_copy(src, dst, out_sem.at[i])
        copy.start()
        writes.append(copy)

    reads[0].wait()
    for a, (rz, vec, out) in enumerate(((rz0, o_v, o_out), (rz1, r_v, r_out), (rz2, s_v, s_out))):
        reads[1 + a].wait()
        tile = own[a]
        for k in range(ZS - 1):
            tile += rz[k, 0:16].astype(F32)
        vec[...] = jnp.concatenate([tile[0:8], tile[8:16]], 1)
        write(a, vec, out)
    tile = own[3]
    for k in range(ZS - 1):
        tile += rz1[k, 16:32].astype(F32)
    line = jnp.broadcast_to(jnp.where(b < NODES // 2, tile[0:1], tile[1:2]), (8, 128))
    lane = lax.broadcasted_iota(jnp.int32, (128, 128), 0)
    want = lax.broadcasted_iota(jnp.int32, (128, 128), 1) + 4 * lax.rem(b, NODES // 2)
    take = (lane == want).astype(F32).astype(BF)
    v0 = line.astype(BF)
    rest = line - v0.astype(F32)
    v1 = rest.astype(BF)
    v2 = (rest - v1.astype(F32)).astype(BF)
    b_v[...] = (nn(v0, take) + nn(v1, take) + nn(v2, take))[0, 0:4]
    write(4, b_v, b_out)

    reads[4].wait()
    late = rcy[HID - 1]
    for k in range(HID - 1):
        late += rcy[k]
    late = jnp.concatenate([late, jnp.zeros((120, 128), F32)], 0).T
    late = jnp.where(lax.rem(y, 2) == 0, late[0:64, :], late[64:128, :])
    reads[5].wait()
    n_v[:, 0:128] = node[:, 0:128] + late
    n_v[:, 128:256] = node[:, 128:256]
    write(3, n_v, n_out)
    for copy in writes:
        copy.wait()


def vm(shape, dtype):
    return pltpu.VMEM(shape, dtype)


def shards(
    latents, cotangent, w_send, w_recv, bias, w_out, fine_sender, fine_receiver, fine_valid,
    send_rows, coarse_slot, coarse_receiver, coarse_valid,
):
    i32 = jnp.int32
    operands = (
        latents, cotangent, w_send, w_recv, bias.reshape(1, H), w_out,
        fine_sender, fine_receiver, fine_valid,
        send_rows[0].T,
        coarse_slot.reshape(1, COARSE), coarse_receiver.reshape(1, COARSE), coarse_valid.reshape(1, COARSE),
    )
    sems = pltpu.SemaphoreType.DMA
    scratch = [vm((16, D), BF)] + [vm(v.shape, v.dtype) for v in operands] + [sems((14,))]
    scratch += [
        vm((32, 128), F32), vm((ZS, 32, 128), BF), vm((ZS, 32, 128), F32), vm((ZS, 32, 128), BF),
        vm((ZS, 32, 128), F32), vm((256, 64), BF), vm((64, 256), BF),
        vm((8, 32, H), BF), vm((8, 32, H), BF), vm((8, 32, D), BF), vm((8, 32, D), BF),
        vm((2 * HALO, D), BF), vm((H, D), BF), vm((D, 640), BF), vm((D, ROWS), BF),
        vm((2 * H, 384), BF), vm((3 * H, ROWS), BF), vm((H, 256), BF),
        vm((3, 384, CH), BF), vm((4, ROWS, CH), BF), vm((256, CH), BF), vm((4, H, CH), F32), vm((4, H, CH), F32),
        vm((384, H), F32), vm((ROWS, 2 * H), F32), vm((256, H), BF),
        vm((8, 32, H), BF), vm((8, 32, H), BF), vm((ZS, 16, 128), BF), vm((ZS, 16, 128), BF),
        vm((2 * HALO, H), BF), vm((2 * HALO, H), BF),
    ]
    scratch += [vm((2, XS, t, 16, 128), BF) for t in TILES]
    scratch += [vm((XS, t, 16, 128), BF) for t in TILES]
    scratch += [vm((XS, t, 16, 128), BF) for t in TILES]
    scratch += [vm((XS - 1, t, 16, 128), BF) for t in TILES]
    scratch += [vm((ZS, 16, 128), F32), vm((4, 16, 128), F32)]
    scratch += [vm((ZS, 16 * (t - 7), 128), BF) for t in TILES]
    scratch += [
        vm((HID, 64, ROWS), F32), vm((HID, 64, ROWS), BF), vm((HID - 1, 64, ROWS), BF),
        vm((64, ROWS), F32), vm((HID, 8, 128), F32),
    ]
    scratch += [
        sems((2, 7)), sems((2, 7)), sems((2, 7)), sems((2, 7)), sems((2, 2)), sems((2, 7)), sems((2, 7)), sems((2, 2)), sems((2, 3)), sems((2, 9)), sems((2, 21)),
        sems((2, 7)), sems((2, 7)), sems((3,)),
    ]
    hbm = pl.BlockSpec(memory_space=pltpu.MemorySpace.HBM)
    kept = [
        ((ZS - 1, 16, 128), BF), ((ZS - 1, 32, 128), BF), ((ZS - 1, 16, 128), BF),
        ((4, 16, 128), F32), ((64, ROWS), F32), ((HID, 8, 128), F32),
    ]
    arrived = pl.pallas_call(
        kernel,
        out_shape=[jax.ShapeDtypeStruct(shape, dtype) for shape, dtype in kept],
        in_specs=[hbm] * 13,
        out_specs=[hbm] * 6,
        scratch_shapes=scratch,
        compiler_params=pltpu.CompilerParams(
            collective_id=0, has_side_effects=True, vmem_limit_bytes=64 * 1024 * 1024
        ),
        name="edge_update",
    )(*operands)
    results = [(64, ROWS), (8, H), (8, H), (8, H)]
    out_n, out_s, out_r, out_o, out_b = pl.pallas_call(
        finish,
        out_shape=[jax.ShapeDtypeStruct(shape, F32) for shape in results + [(4,)]],
        in_specs=[hbm] * 6,
        out_specs=[hbm] * 5,
        scratch_shapes=[vm(shape, dtype) for shape, dtype in kept]
        + [vm(shape, F32) for shape in results + [(4,)]]
        + [sems((6,)), sems((5,))],
        compiler_params=pltpu.CompilerParams(vmem_limit_bytes=64 * 1024 * 1024),
        name="finish",
    )(*arrived)
    return out_n.T, out_s, out_r, out_o.T, out_b


def solution(mesh):
    return jax.shard_map(
        shards,
        mesh=mesh,
        in_specs=(
            P("nodes", None), P("nodes", None), P(None, "hid"), P(None, "hid"), P("hid"), P("hid", None),
            P("nodes"), P("nodes"), P("nodes"), P("nodes", None, None), P("nodes"), P("nodes"), P("nodes"),
        ),
        out_specs=(
            P("nodes", "hid"), P("nodes", "hid"), P("nodes", "hid"), P("hid", "nodes"), P(("hid", "nodes")),
        ),
        check_vma=False,
    )
```
